32 devices in a mesh: grp: 2 (over x), seg: 16 (over z, y, core).
Axes of the slice: x: 2, y: 2, z: 4, core: 2. Of those that a mesh axis runs over, the one named last changes fastest.
Arguments:
- strain: float32 [2097152], P(('grp', 'seg')), parts along dimension 0, may hold values from -6 to 6
- gate_mask: int32 [2097152], P(('grp', 'seg')), parts along dimension 0, may hold values 0 or 1
- template_bank: bfloat16 [32, 2, 32768], P('grp', None, 'seg'), parts along dimension 0, may hold values from -6 to 6
Outputs:
- peak_power: float32 [16, 8192], P(None, ('grp', 'seg')), parts along dimension 1
The draws below stay inside these ranges and needn't reach their ends.
There are 2 independent parts, one for each index of `grp`. The reference program is written for one: setup_inputs(seed, part) draws one part's arguments, and reference() takes and returns one part's arrays. A program takes and returns all parts, laid end to end along the dimension named above; each array names one. Nothing has to cross between parts.
All inputs are finite; a program needn't handle non-finite values. No bound on the sum of `gate_mask` on one device may be relied on, other than what follows from the above.
Results may differ from the reference program's by a relative error of at most 0.0003.
Values may be sent and summed in bfloat16 or wider, within the bound.
A program may use at most 128 MiB of HBM per device.

```python
import jax
import jax.numpy as jnp
from jax import lax

RADIX = 256
NFFT = 65536
BLOCK = 32768
TEMPLATES = 16
SAMPLES = 1048576


def place_ends(result, rng, least, largest):
    shape = result.shape
    index_at = [jax.random.randint(jax.random.fold_in(rng, axis), (), 0, shape[axis]) for axis in range(len(shape))]
    result = result.at[tuple(index_at)].set(least)
    longest = shape.index(max(shape))
    index_at[longest] = (index_at[longest] + 1) % shape[longest]
    return result.at[tuple(index_at)].set(largest)


def block_scale(rng, extent, cuts, low, largest):
    gain, own = 1.0, jax.random.fold_in(rng, 6)
    for dim, blocks in cuts:
        draws = jnp.exp(jax.random.uniform(jax.random.fold_in(own, dim), (blocks,), jnp.float32, low / len(cuts), largest / len(cuts)))
        gain = gain * jnp.repeat(draws, extent[dim] // blocks).reshape([-1 if axis == dim else 1 for axis in range(len(extent))])
    return gain


def normal_values(rng, extent, width, bound, split=(), kind=jnp.bfloat16):
    level = block_scale(rng, extent, split, -0.22, 0.18) if split else 1.0
    result = jax.random.normal(rng, extent, jnp.float32) * width * level
    return jnp.minimum(jnp.maximum(result, -bound), bound).astype(kind)


def setup_inputs(seed: int = 0, part: int = 0) -> dict:
    streams_of = jax.random.split(jax.random.key(seed), 4)
    part_keys = jax.random.split(jax.random.fold_in(streams_of[3], part), 4)
    strain = normal_values(part_keys[0], (SAMPLES,), 1.0, 6.0, ((0, 16),), jnp.float32)
    gate_mask = place_ends((jax.random.randint(part_keys[1], (SAMPLES,), 0, 16) < 15).astype(jnp.int32), jax.random.fold_in(part_keys[1], 1), 0, 1)
    template_bank = normal_values(part_keys[2], (TEMPLATES, 2, BLOCK), 1.0, 6.0, ((2, 16),))
    return {"strain": strain, "gate_mask": gate_mask, "template_bank": template_bank}


EPSILON = 1e-06

def reference(strain, gate_mask, template_bank):
    gated = strain * gate_mask.astype(jnp.float32)
    blocks = gated.reshape(-1, BLOCK)
    spectra = jnp.fft.rfft(blocks, n=NFFT, axis=-1)[:, :BLOCK]
    waveform = template_bank.astype(jnp.float32)

    def one_template(row_pair):
        real_part = row_pair[0]
        imag_part = row_pair[1]
        power_sum = jnp.sum(real_part * real_part + imag_part * imag_part)
        norm_scale = 1.0 / jnp.sqrt(BLOCK * power_sum + EPSILON)
        product = spectra * (real_part - 1j * imag_part)[None, :]
        series = jnp.fft.ifft(product, n=NFFT, axis=-1) * NFFT * norm_scale
        carried = jnp.concatenate([jnp.zeros_like(series[:1, BLOCK:]), series[:-1, BLOCK:]], axis=0)
        summed = series[:, :BLOCK] + carried
        power_series = summed.real * summed.real + summed.imag * summed.imag
        return lax.optimization_barrier(jnp.max(power_series.reshape(-1, BLOCK // RADIX, RADIX), axis=-1)).reshape(-1)
    return lax.map(one_template, waveform)
```

```python
import functools
import math

import jax
import jax.numpy as jnp
import ml_dtypes
import numpy as np
from jax import lax
from jax.experimental import pallas as pl
from jax.experimental.pallas import tpu as pltpu
from jax.sharding import PartitionSpec as P

RADIX = 256
HALF = RADIX // 2
BLOCK = 32768
EPSILON = 1e-06
BF16 = jnp.bfloat16
F32 = jnp.float32
VMEM_LIMIT = 48 * 1024 * 1024


def angles(rows, cols, period):
    phase = np.outer(np.arange(rows), np.arange(cols)) % period
    turn = phase * (2.0 * math.pi / period)
    return np.cos(turn), np.sin(turn)


def two_parts(table):
    high = table.astype(ml_dtypes.bfloat16)
    low = (table - high.astype(np.float64)).astype(ml_dtypes.bfloat16)
    return high, low


@functools.cache
def forward_tables():
    cos, sin = angles(HALF, RADIX, RADIX)
    first = np.concatenate([cos, -sin], axis=1)
    cos, sin = angles(RADIX, RADIX, RADIX * RADIX)
    twist = np.stack([cos, -sin]).astype(np.float32)
    cos, sin = angles(HALF, RADIX, RADIX)
    second = np.block([[cos, sin], [-sin, cos]])
    return two_parts(first) + (twist,) + two_parts(second)


@functools.cache
def inverse_tables():
    cos, sin = angles(RADIX, HALF, RADIX)
    first = np.block([[cos, -sin], [sin, cos]])
    cos, sin = angles(RADIX, RADIX, RADIX * RADIX)
    twist = np.stack([cos, sin]).astype(np.float32)
    cos, sin = angles(RADIX, HALF, RADIX)
    second = np.block([[cos, sin], [-sin, cos]])
    return two_parts(first) + (twist,) + two_parts(second)


def split(value):
    high = value.astype(BF16)
    return high, (value - high.astype(F32)).astype(BF16)


def dot(left, right):
    return jnp.dot(left, right, preferred_element_type=F32)


def forward_kernel(g_ref, prev_ref, th_ref, tl_ref, w_ref, uh_ref, ul_ref, x_ref):
    def grid_of(ref, block):
        halves = [ref[pl.ds(block * RADIX + half, HALF, stride=2), :] for half in range(2)]
        return jnp.concatenate([half.T for half in halves], axis=0)

    def first_stage(grid):
        high, low = split(grid)
        return dot(high, th_ref[...]) + dot(low, th_ref[...]) + dot(high, tl_ref[...])

    parity = lax.broadcasted_iota(jnp.int32, (RADIX, 2 * RADIX), 1) % 2
    sign = (1 - 2 * parity).astype(F32)
    blocks = [first_stage(grid_of(prev_ref, 0))]
    blocks += [first_stage(grid_of(g_ref, block)) for block in range(2)]
    for block in range(2):
        both = blocks[block + 1] + sign * blocks[block]
        real, imag = both[:, :RADIX], both[:, RADIX:]
        cos, sin = w_ref[0], w_ref[1]
        turned = jnp.concatenate([real * cos - imag * sin, real * sin + imag * cos], axis=0)
        high, low = split(turned)
        x_ref[block] = dot(uh_ref[...], high) + dot(uh_ref[...], low) + dot(ul_ref[...], high)


def inverse_kernel(h_ref, x_ref, th_ref, tl_ref, w_ref, uh_ref, ul_ref, o_ref):
    index = pl.program_id(0)
    bank_real = h_ref[0, 0].astype(F32)
    bank_imag = h_ref[0, 1].astype(F32)
    power_sum = jnp.sum(bank_real * bank_real + bank_imag * bank_imag)
    scale = 1.0 / (BLOCK * power_sum + EPSILON)
    cos, sin = w_ref[0], w_ref[1]
    peaks = []
    for block in range(2):
        real, imag = x_ref[block, :HALF], x_ref[block, HALF:]
        product = jnp.concatenate(
            [real * bank_real + imag * bank_imag, imag * bank_real - real * bank_imag], axis=0
        )
        high, low = split(product)
        part = dot(th_ref[...], high) + dot(tl_ref[...], high) + dot(th_ref[...], low)
        real, imag = part[:RADIX], part[RADIX:]
        turned = jnp.concatenate([real * cos - imag * sin, real * sin + imag * cos], axis=1)
        high, low = split(turned)
        series = dot(high, uh_ref[...]) + dot(low, uh_ref[...]) + dot(high, ul_ref[...])
        real, imag = series[:, :HALF], series[:, HALF:]
        peaks.append(jnp.max(real * real + imag * imag, axis=0, keepdims=True))
    row = lax.broadcasted_iota(jnp.int32, o_ref.shape, 0)
    o_ref[...] = jnp.where(row == index, jnp.concatenate(peaks, axis=1) * scale, o_ref[...])


def whole(shape):
    return pl.BlockSpec(shape, lambda *_: (0,) * len(shape))


def local(strain, gate_mask, template_bank):
    template_total = template_bank.shape[0]
    gated = (strain * gate_mask.astype(F32)).reshape(-1, 128)
    count = lax.axis_size("seg")
    pairs = [(i, i + 1) for i in range(count - 1)]
    prev = lax.ppermute(gated[-RADIX:], "seg", pairs)
    rows = template_bank.reshape(template_total, 2, -1, RADIX)
    bank = lax.all_gather(rows, "seg", axis=2, tiled=True)
    spectra = pl.pallas_call(
        forward_kernel,
        out_shape=jax.ShapeDtypeStruct((2, RADIX, RADIX), F32),
        compiler_params=pltpu.CompilerParams(vmem_limit_bytes=VMEM_LIMIT),
        cost_estimate=pl.CostEstimate(flops=6 * 120_000_000, bytes_accessed=3_000_000, transcendentals=0),
        name="window_spectra",
    )(gated, prev, *(jnp.asarray(t) for t in forward_tables()))
    tables = [jnp.asarray(t) for t in inverse_tables()]
    return pl.pallas_call(
        inverse_kernel,
        out_shape=jax.ShapeDtypeStruct((template_total, RADIX), F32),
        grid=(template_total,),
        in_specs=[
            pl.BlockSpec((1, 2, HALF, RADIX), lambda k: (k, 0, 0, 0)),
            whole((2, RADIX, RADIX)),
            *(whole(t.shape) for t in tables),
        ],
        out_specs=whole((template_total, RADIX)),
        compiler_params=pltpu.CompilerParams(vmem_limit_bytes=VMEM_LIMIT),
        name="series_peaks",
    )(bank, spectra, *tables)


def solution(mesh):
    in_specs = (P(("grp", "seg")), P(("grp", "seg")), P("grp", None, "seg"))
    out_specs = P(None, ("grp", "seg"))
    return jax.shard_map(local, mesh=mesh, in_specs=in_specs, out_specs=out_specs, check_vma=False)
```

```python
import functools
import math

import jax
import jax.numpy as jnp
import ml_dtypes
import numpy as np
from jax import lax
from jax.experimental import pallas as pl
from jax.experimental.pallas import tpu as pltpu
from jax.sharding import PartitionSpec as P

RADIX = 256
HALF = RADIX // 2
BLOCK = 32768
EPSILON = 1e-06
BF16 = jnp.bfloat16
F32 = jnp.float32
MESH = pl.DeviceIdType.MESH
VMEM_LIMIT = 56 * 1024 * 1024
SEGS = 16
GROUP = 2
GROUPS = 8


def angles(rows, cols, period):
    phase = np.outer(np.arange(rows), np.arange(cols)) % period
    turn = phase * (2.0 * math.pi / period)
    return np.cos(turn), np.sin(turn)


def two_parts(table):
    high = table.astype(ml_dtypes.bfloat16)
    low = (table - high.astype(np.float64)).astype(ml_dtypes.bfloat16)
    return high, low


@functools.cache
def forward_tables():
    cos, sin = angles(HALF, RADIX, RADIX)
    high, low = two_parts(np.concatenate([cos, -sin], axis=1))
    cos, sin = angles(HALF, RADIX, RADIX)
    second = two_parts(np.block([[cos, sin], [-sin, cos]]))
    return high, low, np.concatenate([second[0], second[1], second[0]], axis=1)


@functools.cache
def inverse_tables():
    cos, sin = angles(RADIX, HALF, RADIX)
    first = two_parts(np.block([[cos, -sin], [sin, cos]]))
    cos, sin = angles(RADIX, RADIX, RADIX * RADIX)
    twist = np.stack([cos, sin]).astype(np.float32)
    cos, sin = angles(RADIX, HALF, RADIX)
    second = two_parts(np.block([[cos, sin], [-sin, cos]]))
    return (
        np.concatenate([first[0], first[1], first[0]], axis=1),
        twist,
        np.concatenate([second[0], second[0], second[1]], axis=0),
    )


def split(value):
    high = value.astype(BF16)
    return high, (value - high.astype(F32)).astype(BF16)


def dot(left, right):
    return jnp.dot(left, right, preferred_element_type=F32)


def inverse_kernel(h_ref, x_ref, t_ref, w_ref, u_ref, o_ref):
    index = pl.program_id(0)
    peaks = template_peaks([(h_ref[0, 0], h_ref[0, 1])], x_ref, t_ref, w_ref, u_ref)[0]
    row = lax.broadcasted_iota(jnp.int32, o_ref.shape, 0)
    o_ref[...] = jnp.where(row == index, peaks, o_ref[...])


def template_peaks(banks, x_ref, t_ref, w_ref, u_ref):
    wide = [(real.astype(F32), imag.astype(F32)) for real, imag in banks]
    scales = [
        1.0 / (BLOCK * jnp.sum(real * real + imag * imag) + EPSILON) for real, imag in wide
    ]

    def first(item):
        bank_real, bank_imag = wide[item // 2]
        real, imag = x_ref[item % 2, :HALF], x_ref[item % 2, HALF:]
        high, low = split(
            jnp.concatenate(
                [real * bank_real + imag * bank_imag, imag * bank_real - real * bank_imag], axis=0
            )
        )
        return dot(t_ref[...], jnp.concatenate([high, high, low], axis=0))

    def second(part):
        real, imag = part[:RADIX], part[RADIX:]
        cos, sin = w_ref[0], w_ref[1]
        high, low = split(
            jnp.concatenate([real * cos - imag * sin, real * sin + imag * cos], axis=1)
        )
        return dot(jnp.concatenate([high, low, high], axis=1), u_ref[...])

    def peak(series):
        real, imag = series[:, :HALF], series[:, HALF:]
        return jnp.max(real * real + imag * imag, axis=0, keepdims=True)

    count = 2 * len(banks)
    parts = [first(0)]
    peaks = []
    for item in range(count):
        if item + 1 < count:
            parts.append(first(item + 1))
        peaks.append(peak(second(parts[item])))
    return [
        jnp.concatenate(peaks[2 * i : 2 * i + 2], axis=1) * scales[i] for i in range(len(banks))
    ]


def window_spectra(grids, th_ref, tl_ref, w_ref, u_ref, x_ref):
    def first_stage(grid):
        high, low = split(grid)
        return dot(high, th_ref[...]) + dot(low, th_ref[...]) + dot(high, tl_ref[...])

    parity = lax.broadcasted_iota(jnp.int32, (RADIX, 2 * RADIX), 1) % 2
    sign = (1 - 2 * parity).astype(F32)
    blocks = [first_stage(grid) for grid in grids]
    for block in range(2):
        both = blocks[block + 1] + sign * blocks[block]
        real, imag = both[:, :RADIX], both[:, RADIX:]
        cos, sin = w_ref[0], w_ref[1]
        high, low = split(
            jnp.concatenate([real * cos + imag * sin, imag * cos - real * sin], axis=0)
        )
        x_ref[block] = dot(u_ref[...], jnp.concatenate([high, high, low], axis=0))


def grid_of(ref, start):
    halves = [ref[pl.ds(start + half, HALF, stride=2), :] for half in range(2)]
    return jnp.concatenate([half.T for half in halves], axis=0)


def forward_kernel(g_ref, prev_ref, th_ref, tl_ref, w_ref, u_ref, x_ref):
    grids = [grid_of(prev_ref, 0), grid_of(g_ref, 0), grid_of(g_ref, RADIX)]
    window_spectra(grids, th_ref, tl_ref, w_ref, u_ref, x_ref)


def fused_kernel(
    strain_ref, mask_ref, bank_ref, th_ref, tl_ref, w_ref, fu_ref, t_ref, u_ref, o_ref,
    gated, prev, held, x_ref, prev_sem, own_send, pass_send, recv_sem,
):
    me = lax.axis_index("seg")
    z_peers = [(me + 4 * step) % SEGS for step in range(1, 4)]
    y_peer = me + 2 - 4 * ((me // 2) % 2)
    sibling = me + 1 - 2 * (me % 2)
    last = SEGS - 1

    barrier = pltpu.get_barrier_semaphore()
    for peer in (*z_peers, y_peer, sibling, (me + last) % SEGS):
        pl.semaphore_signal(barrier, inc=1, device_id={"seg": peer}, device_id_type=MESH)

    gated[...] = strain_ref[...] * mask_ref[...].astype(F32)
    held[me] = bank_ref[...]

    pl.semaphore_wait(barrier, 6)

    def prev_copy():
        return pltpu.make_async_remote_copy(
            src_ref=gated.at[pl.ds(RADIX, RADIX)],
            dst_ref=prev,
            send_sem=prev_sem.at[0],
            recv_sem=prev_sem.at[1],
            device_id={"seg": me + 1},
            device_id_type=MESH,
        )

    @pl.when(me < last)
    def _():
        prev_copy().start()

    def chunk_copy(group, chunk, send_sem, peer):
        piece = held.at[chunk, pl.ds(group * GROUP, GROUP)]
        return pltpu.make_async_remote_copy(
            src_ref=piece,
            dst_ref=piece,
            send_sem=send_sem,
            recv_sem=recv_sem.at[group, chunk],
            device_id={"seg": peer},
            device_id_type=MESH,
        )

    def own_copies(group):
        return [
            chunk_copy(group, me, own_send.at[group, i], peer)
            for i, peer in enumerate((*z_peers, y_peer, sibling))
        ]

    def z_chunks():
        return z_peers

    def y_chunks():
        return [(y_peer + 4 * step) % SEGS for step in range(4)]

    def sibling_chunks():
        mine = [(me + 4 * step) % SEGS for step in range(4)] + y_chunks()
        return [chunk + 1 - 2 * (chunk % 2) for chunk in mine]

    def z_copies(group):
        return [
            chunk_copy(group, chunk, pass_send.at[group, 2 * i + j], peer)
            for i, chunk in enumerate(z_chunks())
            for j, peer in enumerate((y_peer, sibling))
        ]

    def y_copies(group):
        return [
            chunk_copy(group, chunk, pass_send.at[group, 6 + i], sibling)
            for i, chunk in enumerate(y_chunks())
        ]

    def arrived(group, chunk):
        chunk_copy(group, chunk, own_send.at[group, 0], sibling).wait_recv()

    def pass_z(group):
        copies = z_copies(group)
        for i, chunk in enumerate(z_chunks()):
            arrived(group, chunk)
            copies[2 * i].start()
            copies[2 * i + 1].start()

    def pass_y(group):
        copies = y_copies(group)
        for i, chunk in enumerate(y_chunks()):
            arrived(group, chunk)
            copies[i].start()

    def start_own(group, carry):
        for copy in own_copies(group):
            copy.start()
        return carry

    lax.fori_loop(0, GROUPS, start_own, 0)
    o_ref[...] = jnp.zeros_like(o_ref)

    @pl.when(me == 0)
    def _():
        prev[...] = jnp.zeros_like(prev)

    pass_z(0)

    @pl.when(me > 0)
    def _():
        prev_copy().wait_recv()

    pass_z(1)
    grids = [grid_of(prev, 0), grid_of(gated, 0), grid_of(gated, RADIX)]
    window_spectra(grids, th_ref, tl_ref, w_ref, fu_ref, x_ref)
    pass_y(0)

    def step(group, carry):
        @pl.when(group + 2 < GROUPS)
        def _():
            pass_z(group + 2)

        @pl.when(group + 1 < GROUPS)
        def _():
            pass_y(group + 1)

        for chunk in sibling_chunks():
            arrived(group, chunk)
        banks = []
        for item in range(GROUP):
            rows = held[:, group * GROUP + item]
            banks.append(
                (rows[:, : rows.shape[1] // 2], rows[:, rows.shape[1] // 2 :])
            )
        banks = [
            (real.astype(F32).reshape(HALF, RADIX), imag.astype(F32).reshape(HALF, RADIX))
            for real, imag in banks
        ]
        row = lax.broadcasted_iota(jnp.int32, o_ref.shape, 0)
        total = o_ref[...]
        for item, peaks in enumerate(template_peaks(banks, x_ref, t_ref, w_ref, u_ref)):
            total = jnp.where(row == group * GROUP + item, peaks, total)
        o_ref[...] = total
        return carry

    lax.fori_loop(0, GROUPS, step, 0)

    def finish(group, carry):
        for copy in own_copies(group) + z_copies(group) + y_copies(group):
            copy.wait_send()
        return carry

    lax.fori_loop(0, GROUPS, finish, 0)

    @pl.when(me < last)
    def _():
        prev_copy().wait_send()


def fused(strain, gate_mask, rows):
    template_total = rows.shape[0]
    th, tl, fu = (jnp.asarray(t) for t in forward_tables())
    t3, twist, u3 = (jnp.asarray(t) for t in inverse_tables())
    vmem = pl.BlockSpec(memory_space=pltpu.VMEM)
    return pl.pallas_call(
        fused_kernel,
        out_shape=jax.ShapeDtypeStruct((template_total, RADIX), F32),
        in_specs=[vmem] * 9,
        out_specs=vmem,
        scratch_shapes=[
            pltpu.VMEM((2 * RADIX, 128), F32),
            pltpu.VMEM((RADIX, 128), F32),
            pltpu.VMEM((SEGS, *rows.shape), BF16),
            pltpu.VMEM((2, RADIX, RADIX), F32),
            pltpu.SemaphoreType.DMA((2,)),
            pltpu.SemaphoreType.DMA((GROUPS, 5)),
            pltpu.SemaphoreType.DMA((GROUPS, 10)),
            pltpu.SemaphoreType.DMA((GROUPS, SEGS)),
        ],
        compiler_params=pltpu.CompilerParams(
            vmem_limit_bytes=VMEM_LIMIT, collective_id=0, has_side_effects=True
        ),
        name="matched_filter",
    )(strain.reshape(-1, 128), gate_mask.reshape(-1, 128), rows, th, tl, twist, fu, t3, u3)


def whole(shape):
    return pl.BlockSpec(shape, lambda *_: (0,) * len(shape))


def local(strain, gate_mask, template_bank):
    template_total = template_bank.shape[0]
    count = lax.axis_size("seg")
    if count == SEGS and template_total == GROUP * GROUPS:
        return fused(strain, gate_mask, template_bank.reshape(template_total, -1, RADIX))
    gated = (strain * gate_mask.astype(F32)).reshape(-1, 128)
    pairs = [(i, i + 1) for i in range(count - 1)]
    prev = lax.ppermute(gated[-RADIX:], "seg", pairs)
    rows = template_bank.reshape(template_total, 2, -1, RADIX)
    bank = lax.all_gather(rows, "seg", axis=2, tiled=True)
    th, tl, fu = (jnp.asarray(t) for t in forward_tables())
    t3, twist, u3 = (jnp.asarray(t) for t in inverse_tables())
    params = pltpu.CompilerParams(vmem_limit_bytes=VMEM_LIMIT)
    spectra = pl.pallas_call(
        forward_kernel,
        out_shape=jax.ShapeDtypeStruct((2, RADIX, RADIX), F32),
        compiler_params=params,
        name="window_spectra",
    )(gated, prev, th, tl, twist, fu)
    tables = (t3, twist, u3)
    return pl.pallas_call(
        inverse_kernel,
        out_shape=jax.ShapeDtypeStruct((template_total, RADIX), F32),
        grid=(template_total,),
        in_specs=[
            pl.BlockSpec((1, 2, HALF, RADIX), lambda k: (k, 0, 0, 0)),
            whole((2, RADIX, RADIX)),
            *(whole(t.shape) for t in tables),
        ],
        out_specs=whole((template_total, RADIX)),
        compiler_params=params,
        name="series_peaks",
    )(bank, spectra, *tables)


def solution(mesh):
    in_specs = (P(("grp", "seg")), P(("grp", "seg")), P("grp", None, "seg"))
    out_specs = P(None, ("grp", "seg"))
    return jax.shard_map(local, mesh=mesh, in_specs=in_specs, out_specs=out_specs, check_vma=False)
```

```python
import functools
import math

import jax
import jax.numpy as jnp
import ml_dtypes
import numpy as np
from jax import lax
from jax.experimental import pallas as pl
from jax.experimental.pallas import tpu as pltpu
from jax.sharding import PartitionSpec as P

RADIX = 256
HALF = RADIX // 2
BLOCK = 32768
EPSILON = 1e-06
BF16 = jnp.bfloat16
F32 = jnp.float32
MESH = pl.DeviceIdType.MESH
VMEM_LIMIT = 56 * 1024 * 1024
SEGS = 16
GROUP = 2
GROUPS = 8
AHEAD = 4
TABLES = 6


def angles(rows, cols, period):
    phase = np.outer(np.arange(rows), np.arange(cols)) % period
    turn = phase * (2.0 * math.pi / period)
    return np.cos(turn), np.sin(turn)


def two_parts(table):
    high = table.astype(ml_dtypes.bfloat16)
    low = (table - high.astype(np.float64)).astype(ml_dtypes.bfloat16)
    return high, low


@functools.cache
def forward_tables():
    cos, sin = angles(HALF, RADIX, RADIX)
    high, low = two_parts(np.concatenate([cos, -sin], axis=1))
    cos, sin = angles(HALF, RADIX, RADIX)
    second = two_parts(np.block([[cos, sin], [-sin, cos]]))
    return high, low, np.concatenate([second[0], second[1], second[0]], axis=1)


@functools.cache
def inverse_tables():
    cos, sin = angles(RADIX, HALF, RADIX)
    first = two_parts(np.block([[cos, -sin], [sin, cos]]))
    cos, sin = angles(RADIX, RADIX, RADIX * RADIX)
    twist = np.stack([cos, sin]).astype(np.float32)
    cos, sin = angles(RADIX, HALF, RADIX)
    second = two_parts(np.block([[cos, sin], [-sin, cos]]))
    return (
        np.concatenate([first[0], first[1], first[0]], axis=1),
        twist,
        np.concatenate([second[0], second[0], second[1]], axis=0),
    )


def split(value):
    high = value.astype(BF16)
    return high, (value - high.astype(F32)).astype(BF16)


def dot(left, right):
    return jnp.dot(left, right, preferred_element_type=F32)


def inverse_kernel(h_ref, x_ref, t_ref, w_ref, u_ref, o_ref, part_ref, scale_ref):
    index = pl.program_id(0)
    bank_real, bank_imag = h_ref[0, 0].astype(F32), h_ref[0, 1].astype(F32)
    first_product(bank_real, bank_imag, x_ref, t_ref, part_ref, scale_ref)
    peaks = second_product(part_ref, scale_ref, w_ref, u_ref)
    row = lax.broadcasted_iota(jnp.int32, o_ref.shape, 0)
    o_ref[...] = jnp.where(row == index, peaks, o_ref[...])


def first_product(bank_real, bank_imag, x_ref, t_ref, part_ref, scale_ref):
    scale = 1.0 / (BLOCK * jnp.sum(bank_real * bank_real + bank_imag * bank_imag) + EPSILON)
    scale_ref[...] = jnp.full(scale_ref.shape, scale, F32)
    highs, lows = [], []
    for block in range(2):
        real, imag = x_ref[block, :HALF], x_ref[block, HALF:]
        high, low = split(
            jnp.concatenate(
                [real * bank_real + imag * bank_imag, imag * bank_real - real * bank_imag], axis=0
            )
        )
        highs.append(high)
        lows.append(low)
    high, low = jnp.concatenate(highs, axis=1), jnp.concatenate(lows, axis=1)
    part_ref[...] = dot(t_ref[...], jnp.concatenate([high, high, low], axis=0))


def second_product(part_ref, scale_ref, w_ref, u_ref):
    cos, sin = w_ref[0], w_ref[1]
    rows = []
    for block in range(2):
        columns = slice(block * RADIX, (block + 1) * RADIX)
        real, imag = part_ref[:RADIX, columns], part_ref[RADIX:, columns]
        high, low = split(
            jnp.concatenate([real * cos - imag * sin, real * sin + imag * cos], axis=1)
        )
        rows.append(jnp.concatenate([high, low, high], axis=1))
    series = dot(jnp.concatenate(rows, axis=0), u_ref[...])
    real, imag = series[:, :HALF], series[:, HALF:]
    power = real * real + imag * imag
    peaks = [
        jnp.max(power[block * RADIX : (block + 1) * RADIX], axis=0, keepdims=True)
        for block in range(2)
    ]
    return jnp.concatenate(peaks, axis=1) * scale_ref[...]


def window_spectra(grids, th_ref, tl_ref, w_ref, u_ref, x_ref):
    def first_stage(grid):
        high, low = split(grid)
        return dot(high, th_ref[...]) + dot(low, th_ref[...]) + dot(high, tl_ref[...])

    parity = lax.broadcasted_iota(jnp.int32, (RADIX, 2 * RADIX), 1) % 2
    sign = (1 - 2 * parity).astype(F32)
    blocks = [first_stage(grid) for grid in grids]
    for block in range(2):
        both = blocks[block + 1] + sign * blocks[block]
        real, imag = both[:, :RADIX], both[:, RADIX:]
        cos, sin = w_ref[0], w_ref[1]
        high, low = split(
            jnp.concatenate([real * cos + imag * sin, imag * cos - real * sin], axis=0)
        )
        x_ref[block] = dot(u_ref[...], jnp.concatenate([high, high, low], axis=0))


def grid_of(ref, start):
    halves = [ref[pl.ds(start + half, HALF, stride=2), :] for half in range(2)]
    return jnp.concatenate([half.T for half in halves], axis=0)


def forward_kernel(g_ref, prev_ref, th_ref, tl_ref, w_ref, u_ref, x_ref):
    grids = [grid_of(prev_ref, 0), grid_of(g_ref, 0), grid_of(g_ref, RADIX)]
    window_spectra(grids, th_ref, tl_ref, w_ref, u_ref, x_ref)


def fused_kernel(
    strain_ref, mask_ref, bank_ref, *refs,
):
    outside, refs = refs[:TABLES], refs[TABLES:]
    o_ref, gated, prev, held, x_ref, part_a, part_b, scale_a, scale_b, *refs = refs
    prev_sem, own_send, pass_send, recv_sem, table_sem, *tables = refs
    th_ref, tl_ref, w_ref, fu_ref, t_ref, u_ref = tables
    me = lax.axis_index("seg")
    z_peers = [(me + 4 * step) % SEGS for step in range(1, 4)]
    y_peer = me + 2 - 4 * ((me // 2) % 2)
    sibling = me + 1 - 2 * (me % 2)
    last = SEGS - 1

    barrier = pltpu.get_barrier_semaphore()
    for peer in (*z_peers, y_peer, sibling, (me + last) % SEGS):
        pl.semaphore_signal(barrier, inc=1, device_id={"seg": peer}, device_id_type=MESH)

    table_copies = [
        pltpu.make_async_copy(outside[i], tables[i], table_sem.at[i]) for i in range(TABLES)
    ]
    for copy in table_copies:
        copy.start()
    gated[...] = strain_ref[...] * mask_ref[...].astype(F32)
    held[me] = bank_ref[...]

    pl.semaphore_wait(barrier, 6)

    def prev_copy():
        return pltpu.make_async_remote_copy(
            src_ref=gated.at[pl.ds(RADIX, RADIX)],
            dst_ref=prev,
            send_sem=prev_sem.at[0],
            recv_sem=prev_sem.at[1],
            device_id={"seg": me + 1},
            device_id_type=MESH,
        )

    @pl.when(me < last)
    def _():
        prev_copy().start()

    def chunk_copy(group, chunk, send_sem, peer):
        piece = held.at[chunk, pl.ds(group * GROUP, GROUP)]
        return pltpu.make_async_remote_copy(
            src_ref=piece,
            dst_ref=piece,
            send_sem=send_sem,
            recv_sem=recv_sem.at[group, chunk],
            device_id={"seg": peer},
            device_id_type=MESH,
        )

    def own_copies(group):
        return [
            chunk_copy(group, me, own_send.at[group, i], peer)
            for i, peer in enumerate((*z_peers, y_peer, sibling))
        ]

    def z_chunks():
        return z_peers

    def y_chunks():
        return [(y_peer + 4 * step) % SEGS for step in range(4)]

    def sibling_chunks():
        mine = [(me + 4 * step) % SEGS for step in range(4)] + y_chunks()
        return [chunk + 1 - 2 * (chunk % 2) for chunk in mine]

    def z_copies(group):
        return [
            chunk_copy(group, chunk, pass_send.at[group, 2 * i + j], peer)
            for i, chunk in enumerate(z_chunks())
            for j, peer in enumerate((y_peer, sibling))
        ]

    def y_copies(group):
        return [
            chunk_copy(group, chunk, pass_send.at[group, 6 + i], sibling)
            for i, chunk in enumerate(y_chunks())
        ]

    def arrived(group, chunk):
        chunk_copy(group, chunk, own_send.at[group, 0], sibling).wait_recv()

    def pass_z(group):
        copies = z_copies(group)
        for i, chunk in enumerate(z_chunks()):
            arrived(group, chunk)
            copies[2 * i].start()
            copies[2 * i + 1].start()

    def pass_y(group):
        copies = y_copies(group)
        for i, chunk in enumerate(y_chunks()):
            arrived(group, chunk)
            copies[i].start()

    def start_own(group, carry):
        for copy in own_copies(group):
            copy.start()
        return carry

    lax.fori_loop(0, AHEAD, start_own, 0)
    o_ref[...] = jnp.zeros_like(o_ref)

    @pl.when(me == 0)
    def _():
        prev[...] = jnp.zeros_like(prev)

    pass_z(0)

    @pl.when(me > 0)
    def _():
        prev_copy().wait_recv()

    for copy in table_copies:
        copy.wait()
    pass_z(1)
    grids = [grid_of(prev, 0), grid_of(gated, 0), grid_of(gated, RADIX)]
    window_spectra(grids, th_ref, tl_ref, w_ref, fu_ref, x_ref)
    pass_y(0)

    def first(template, part_ref, scale_ref):
        rows = held[:, template].astype(F32)
        half = rows.shape[1] // 2
        bank_real = rows[:, :half].reshape(HALF, RADIX)
        bank_imag = rows[:, half:].reshape(HALF, RADIX)
        first_product(bank_real, bank_imag, x_ref, t_ref, part_ref, scale_ref)

    def second(template, part_ref, scale_ref):
        peaks = second_product(part_ref, scale_ref, w_ref, u_ref)
        row = lax.broadcasted_iota(jnp.int32, o_ref.shape, 0)
        o_ref[...] = jnp.where(row == template, peaks, o_ref[...])

    def all_arrived(group):
        for chunk in sibling_chunks():
            arrived(group, chunk)

    def step(group, carry):
        @pl.when(group + AHEAD < GROUPS)
        def _():
            start_own(group + AHEAD, 0)

        @pl.when(group + 2 < GROUPS)
        def _():
            pass_z(group + 2)

        pass_y(group + 1)
        first(2 * group + 1, part_b, scale_b)
        second(2 * group, part_a, scale_a)
        all_arrived(group + 1)
        first(2 * group + 2, part_a, scale_a)
        second(2 * group + 1, part_b, scale_b)
        return carry

    all_arrived(0)
    first(0, part_a, scale_a)
    lax.fori_loop(0, GROUPS - 1, step, 0)
    first(2 * GROUPS - 1, part_b, scale_b)
    second(2 * GROUPS - 2, part_a, scale_a)
    second(2 * GROUPS - 1, part_b, scale_b)

    def finish(group, carry):
        for copy in own_copies(group) + z_copies(group) + y_copies(group):
            copy.wait_send()
        return carry

    lax.fori_loop(0, GROUPS, finish, 0)

    @pl.when(me < last)
    def _():
        prev_copy().wait_send()


def fused(strain, gate_mask, rows):
    template_total = rows.shape[0]
    th, tl, fu = forward_tables()
    t3, twist, u3 = inverse_tables()
    tables = [jnp.asarray(t) for t in (th, tl, twist, fu, t3, u3)]
    vmem = pl.BlockSpec(memory_space=pltpu.VMEM)
    return pl.pallas_call(
        fused_kernel,
        out_shape=jax.ShapeDtypeStruct((template_total, RADIX), F32),
        in_specs=[vmem] * 3 + [pl.BlockSpec(memory_space=pl.ANY)] * TABLES,
        out_specs=vmem,
        scratch_shapes=[
            pltpu.VMEM((2 * RADIX, 128), F32),
            pltpu.VMEM((RADIX, 128), F32),
            pltpu.VMEM((SEGS, *rows.shape), BF16),
            pltpu.VMEM((2, RADIX, RADIX), F32),
            *[pltpu.VMEM((2 * RADIX, 2 * RADIX), F32)] * 2,
            *[pltpu.VMEM((1, RADIX), F32)] * 2,
            pltpu.SemaphoreType.DMA((2,)),
            pltpu.SemaphoreType.DMA((GROUPS, 5)),
            pltpu.SemaphoreType.DMA((GROUPS, 10)),
            pltpu.SemaphoreType.DMA((GROUPS, SEGS)),
            pltpu.SemaphoreType.DMA((TABLES,)),
            *(pltpu.VMEM(table.shape, table.dtype) for table in tables),
        ],
        compiler_params=pltpu.CompilerParams(
            vmem_limit_bytes=VMEM_LIMIT, collective_id=0, has_side_effects=True
        ),
        name="matched_filter",
    )(strain.reshape(-1, 128), gate_mask.reshape(-1, 128), rows, *tables)


def whole(shape):
    return pl.BlockSpec(shape, lambda *_: (0,) * len(shape))


def local(strain, gate_mask, template_bank):
    template_total = template_bank.shape[0]
    count = lax.axis_size("seg")
    if count == SEGS and template_total == GROUP * GROUPS:
        return fused(strain, gate_mask, template_bank.reshape(template_total, -1, RADIX))
    gated = (strain * gate_mask.astype(F32)).reshape(-1, 128)
    pairs = [(i, i + 1) for i in range(count - 1)]
    prev = lax.ppermute(gated[-RADIX:], "seg", pairs)
    rows = template_bank.reshape(template_total, 2, -1, RADIX)
    bank = lax.all_gather(rows, "seg", axis=2, tiled=True)
    th, tl, fu = (jnp.asarray(t) for t in forward_tables())
    t3, twist, u3 = (jnp.asarray(t) for t in inverse_tables())
    params = pltpu.CompilerParams(vmem_limit_bytes=VMEM_LIMIT)
    spectra = pl.pallas_call(
        forward_kernel,
        out_shape=jax.ShapeDtypeStruct((2, RADIX, RADIX), F32),
        compiler_params=params,
        name="window_spectra",
    )(gated, prev, th, tl, twist, fu)
    tables = (t3, twist, u3)
    return pl.pallas_call(
        inverse_kernel,
        out_shape=jax.ShapeDtypeStruct((template_total, RADIX), F32),
        grid=(template_total,),
        in_specs=[
            pl.BlockSpec((1, 2, HALF, RADIX), lambda k: (k, 0, 0, 0)),
            whole((2, RADIX, RADIX)),
            *(whole(t.shape) for t in tables),
        ],
        out_specs=whole((template_total, RADIX)),
        scratch_shapes=[pltpu.VMEM((2 * RADIX, 2 * RADIX), F32), pltpu.VMEM((1, RADIX), F32)],
        compiler_params=params,
        name="series_peaks",
    )(bank, spectra, *tables)


def solution(mesh):
    in_specs = (P(("grp", "seg")), P(("grp", "seg")), P("grp", None, "seg"))
    out_specs = P(None, ("grp", "seg"))
    return jax.shard_map(local, mesh=mesh, in_specs=in_specs, out_specs=out_specs, check_vma=False)
```

```python
import functools
import math

import jax
import jax.numpy as jnp
import ml_dtypes
import numpy as np
from jax import lax
from jax.experimental import pallas as pl
from jax.experimental.pallas import tpu as pltpu
from jax.sharding import PartitionSpec as P

RADIX = 256
HALF = RADIX // 2
BLOCK = 32768
EPSILON = 1e-06
BF16 = jnp.bfloat16
F32 = jnp.float32
F8 = jnp.float8_e4m3fn
LIFT = 4096.0
NARROW = 16.0
SHRINK = 128.0
TOP = 16.0
MESH = pl.DeviceIdType.MESH
VMEM_LIMIT = 56 * 1024 * 1024
SEGS = 16
GROUP = 2
GROUPS = 8
AHEAD = 4
TABLES = 8


def angles(rows, cols, period):
    phase = np.outer(np.arange(rows), np.arange(cols)) % period
    turn = phase * (2.0 * math.pi / period)
    return np.cos(turn), np.sin(turn)


def two_parts(table):
    high = table.astype(ml_dtypes.bfloat16)
    low = (table - high.astype(np.float64)).astype(ml_dtypes.bfloat16)
    return high, low


@functools.cache
def forward_tables():
    cos, sin = angles(HALF, RADIX, RADIX)
    high, low = two_parts(np.concatenate([cos, -sin], axis=1))
    cos, sin = angles(HALF, RADIX, RADIX)
    second = two_parts(np.block([[cos, sin], [-sin, cos]]))
    return high, low, np.concatenate([second[0], second[1], second[0]], axis=1)


@functools.cache
def inverse_tables():
    cos, sin = angles(RADIX, HALF, RADIX)
    high, low = two_parts(np.block([[cos, -sin], [sin, cos]]))
    first = (high.astype(np.float64) * LIFT).astype(ml_dtypes.bfloat16)
    first_rest = np.concatenate([small(high.astype(np.float64) * NARROW), small(low.astype(np.float64) * LIFT)], axis=1)
    cos, sin = angles(RADIX, RADIX, RADIX * RADIX)
    twist = np.stack([cos, sin]).astype(np.float32)
    cos, sin = angles(RADIX, HALF, RADIX)
    high, low = two_parts(np.block([[cos, sin], [-sin, cos]]))
    second = (high.astype(np.float64) * LIFT).astype(ml_dtypes.bfloat16)
    second_rest = np.concatenate([small(high.astype(np.float64) * NARROW), small(low.astype(np.float64) * LIFT)], axis=0)
    return first, first_rest, twist, second, second_rest


def small(table):
    return table.astype(np.float64).astype(ml_dtypes.float8_e4m3fn)


def split(value):
    high = value.astype(BF16)
    return high, (value - high.astype(F32)).astype(BF16)


def split_small(value):
    high = value.astype(BF16)
    rest = ((value - high.astype(F32)) * (LIFT / NARROW)).astype(F8)
    return high, rest, value.astype(F8)


def dot(left, right):
    return jnp.dot(left, right, preferred_element_type=F32)


def inverse_kernel(h_ref, x_ref, gain_ref, t_ref, tr_ref, w_ref, u_ref, ur_ref, o_ref, part_ref, scale_ref):
    index = pl.program_id(0)
    bank_real, bank_imag = h_ref[0, 0].astype(F32), h_ref[0, 1].astype(F32)
    first_product(bank_real, bank_imag, x_ref, t_ref, tr_ref, part_ref, scale_ref)
    peaks = second_product(part_ref, scale_ref, gain_ref, w_ref, u_ref, ur_ref)
    row = lax.broadcasted_iota(jnp.int32, o_ref.shape, 0)
    o_ref[...] = jnp.where(row == index, peaks, o_ref[...])


def first_product(bank_real, bank_imag, x_ref, t_ref, tr_ref, part_ref, scale_ref):
    scale = 1.0 / (BLOCK * jnp.sum(bank_real * bank_real + bank_imag * bank_imag) + EPSILON)
    scale_ref[...] = jnp.full(scale_ref.shape, scale, F32)
    pieces = []
    for block in range(2):
        real, imag = x_ref[block, :HALF], x_ref[block, HALF:]
        pieces.append(
            split_small(
                jnp.concatenate(
                    [real * bank_real + imag * bank_imag, imag * bank_real - real * bank_imag],
                    axis=0,
                )
            )
        )
    high, rest, value = (jnp.concatenate(pair, axis=1) for pair in zip(*pieces))
    part_ref[...] = dot(t_ref[...], high) + dot(
        tr_ref[...], jnp.concatenate([rest, value], axis=0)
    )


def second_product(part_ref, scale_ref, gain_ref, w_ref, u_ref, ur_ref):
    cos, sin = w_ref[0] * (1.0 / (LIFT * SHRINK)), w_ref[1] * (1.0 / (LIFT * SHRINK))
    pieces = []
    for block in range(2):
        columns = slice(block * RADIX, (block + 1) * RADIX)
        real, imag = part_ref[:RADIX, columns], part_ref[RADIX:, columns]
        high, rest, value = split_small(
            jnp.concatenate([real * cos - imag * sin, real * sin + imag * cos], axis=1)
        )
        pieces.append((high, jnp.concatenate([rest, value], axis=1)))
    high, small_parts = (jnp.concatenate(pair, axis=0) for pair in zip(*pieces))
    series = dot(high, u_ref[...]) + dot(small_parts, ur_ref[...])
    real, imag = series[:, :HALF], series[:, HALF:]
    power = real * real + imag * imag
    peaks = [
        jnp.max(power[block * RADIX : (block + 1) * RADIX], axis=0, keepdims=True)
        for block in range(2)
    ]
    gain = gain_ref[...]
    both = jnp.concatenate(peaks, axis=1) * ((SHRINK / LIFT) ** 2 * scale_ref[...])
    return both * gain * gain


def window_spectra(grids, th_ref, tl_ref, w_ref, u_ref, x_ref, gain_ref):
    def first_stage(grid):
        high, low = split(grid)
        return dot(high, th_ref[...]) + dot(low, th_ref[...]) + dot(high, tl_ref[...])

    parity = lax.broadcasted_iota(jnp.int32, (RADIX, 2 * RADIX), 1) % 2
    sign = (1 - 2 * parity).astype(F32)
    blocks = [first_stage(grid) for grid in grids]
    for block in range(2):
        both = blocks[block + 1] + sign * blocks[block]
        real, imag = both[:, :RADIX], both[:, RADIX:]
        cos, sin = w_ref[0], w_ref[1]
        high, low = split(
            jnp.concatenate([real * cos + imag * sin, imag * cos - real * sin], axis=0)
        )
        spectra = dot(u_ref[...], jnp.concatenate([high, high, low], axis=0))
        gain = jnp.maximum(jnp.max(jnp.abs(spectra)), 1e-30) * (1.0 / TOP)
        gain_ref[:, block * HALF : (block + 1) * HALF] = jnp.full((1, HALF), gain, F32)
        x_ref[block] = spectra * (1.0 / gain)


def grid_of(ref, start):
    halves = [ref[pl.ds(start + half, HALF, stride=2), :] for half in range(2)]
    return jnp.concatenate([half.T for half in halves], axis=0)


def forward_kernel(g_ref, prev_ref, th_ref, tl_ref, w_ref, u_ref, x_ref, gain_ref):
    grids = [grid_of(prev_ref, 0), grid_of(g_ref, 0), grid_of(g_ref, RADIX)]
    window_spectra(grids, th_ref, tl_ref, w_ref, u_ref, x_ref, gain_ref)


def fused_kernel(
    strain_ref, mask_ref, bank_ref, *refs,
):
    outside, refs = refs[:TABLES], refs[TABLES:]
    o_ref, gated, prev, held, x_ref, gain_ref, part_a, part_b, scale_a, scale_b, *refs = refs
    prev_sem, own_send, pass_send, recv_sem, table_sem, *tables = refs
    th_ref, tl_ref, fu_ref, t_ref, tr_ref, w_ref, u_ref, ur_ref = tables
    me = lax.axis_index("seg")
    z_peers = [(me + 4 * step) % SEGS for step in range(1, 4)]
    y_peer = me + 2 - 4 * ((me // 2) % 2)
    sibling = me + 1 - 2 * (me % 2)
    last = SEGS - 1

    barrier = pltpu.get_barrier_semaphore()
    for peer in (*z_peers, y_peer, sibling, (me + last) % SEGS):
        pl.semaphore_signal(barrier, inc=1, device_id={"seg": peer}, device_id_type=MESH)

    table_copies = [
        pltpu.make_async_copy(outside[i], tables[i], table_sem.at[i]) for i in range(TABLES)
    ]
    for copy in table_copies:
        copy.start()
    gated[...] = strain_ref[...] * mask_ref[...].astype(F32)
    held[me] = bank_ref[...]

    pl.semaphore_wait(barrier, 6)

    def prev_copy():
        return pltpu.make_async_remote_copy(
            src_ref=gated.at[pl.ds(RADIX, RADIX)],
            dst_ref=prev,
            send_sem=prev_sem.at[0],
            recv_sem=prev_sem.at[1],
            device_id={"seg": me + 1},
            device_id_type=MESH,
        )

    @pl.when(me < last)
    def _():
        prev_copy().start()

    def chunk_copy(group, chunk, send_sem, peer):
        piece = held.at[chunk, pl.ds(group * GROUP, GROUP)]
        return pltpu.make_async_remote_copy(
            src_ref=piece,
            dst_ref=piece,
            send_sem=send_sem,
            recv_sem=recv_sem.at[group, chunk],
            device_id={"seg": peer},
            device_id_type=MESH,
        )

    def own_copies(group):
        return [
            chunk_copy(group, me, own_send.at[group, i], peer)
            for i, peer in enumerate((*z_peers, y_peer, sibling))
        ]

    def z_chunks():
        return z_peers

    def y_chunks():
        return [(y_peer + 4 * step) % SEGS for step in range(4)]

    def sibling_chunks():
        mine = [(me + 4 * step) % SEGS for step in range(4)] + y_chunks()
        return [chunk + 1 - 2 * (chunk % 2) for chunk in mine]

    def z_copies(group):
        return [
            chunk_copy(group, chunk, pass_send.at[group, 2 * i + j], peer)
            for i, chunk in enumerate(z_chunks())
            for j, peer in enumerate((y_peer, sibling))
        ]

    def y_copies(group):
        return [
            chunk_copy(group, chunk, pass_send.at[group, 6 + i], sibling)
            for i, chunk in enumerate(y_chunks())
        ]

    def arrived(group, chunk):
        chunk_copy(group, chunk, own_send.at[group, 0], sibling).wait_recv()

    def pass_z(group):
        copies = z_copies(group)
        for i, chunk in enumerate(z_chunks()):
            arrived(group, chunk)
            copies[2 * i].start()
            copies[2 * i + 1].start()

    def pass_y(group):
        copies = y_copies(group)
        for i, chunk in enumerate(y_chunks()):
            arrived(group, chunk)
            copies[i].start()

    def start_own(group, carry):
        for copy in own_copies(group):
            copy.start()
        return carry

    lax.fori_loop(0, AHEAD, start_own, 0)
    o_ref[...] = jnp.zeros_like(o_ref)

    @pl.when(me == 0)
    def _():
        prev[...] = jnp.zeros_like(prev)

    pass_z(0)

    @pl.when(me > 0)
    def _():
        prev_copy().wait_recv()

    for copy in table_copies:
        copy.wait()
    pass_z(1)
    grids = [grid_of(prev, 0), grid_of(gated, 0), grid_of(gated, RADIX)]
    window_spectra(grids, th_ref, tl_ref, w_ref, fu_ref, x_ref, gain_ref)
    pass_y(0)

    def first(template, part_ref, scale_ref):
        rows = held[:, template].astype(F32)
        half = rows.shape[1] // 2
        bank_real = rows[:, :half].reshape(HALF, RADIX)
        bank_imag = rows[:, half:].reshape(HALF, RADIX)
        first_product(bank_real, bank_imag, x_ref, t_ref, tr_ref, part_ref, scale_ref)

    def second(template, part_ref, scale_ref):
        peaks = second_product(part_ref, scale_ref, gain_ref, w_ref, u_ref, ur_ref)
        row = lax.broadcasted_iota(jnp.int32, o_ref.shape, 0)
        o_ref[...] = jnp.where(row == template, peaks, o_ref[...])

    def all_arrived(group):
        for chunk in sibling_chunks():
            arrived(group, chunk)

    def step(group, carry):
        @pl.when(group + AHEAD < GROUPS)
        def _():
            start_own(group + AHEAD, 0)

        @pl.when(group + 2 < GROUPS)
        def _():
            pass_z(group + 2)

        pass_y(group + 1)
        first(2 * group + 1, part_b, scale_b)
        second(2 * group, part_a, scale_a)
        all_arrived(group + 1)
        first(2 * group + 2, part_a, scale_a)
        second(2 * group + 1, part_b, scale_b)
        return carry

    all_arrived(0)
    first(0, part_a, scale_a)
    lax.fori_loop(0, GROUPS - 1, step, 0)
    first(2 * GROUPS - 1, part_b, scale_b)
    second(2 * GROUPS - 2, part_a, scale_a)
    second(2 * GROUPS - 1, part_b, scale_b)

    def finish(group, carry):
        for copy in own_copies(group) + z_copies(group) + y_copies(group):
            copy.wait_send()
        return carry

    lax.fori_loop(0, GROUPS, finish, 0)

    @pl.when(me < last)
    def _():
        prev_copy().wait_send()


def fused(strain, gate_mask, rows):
    template_total = rows.shape[0]
    tables = [jnp.asarray(t) for t in (*forward_tables(), *inverse_tables())]
    vmem = pl.BlockSpec(memory_space=pltpu.VMEM)
    return pl.pallas_call(
        fused_kernel,
        out_shape=jax.ShapeDtypeStruct((template_total, RADIX), F32),
        in_specs=[vmem] * 3 + [pl.BlockSpec(memory_space=pl.ANY)] * TABLES,
        out_specs=vmem,
        scratch_shapes=[
            pltpu.VMEM((2 * RADIX, 128), F32),
            pltpu.VMEM((RADIX, 128), F32),
            pltpu.VMEM((SEGS, *rows.shape), BF16),
            pltpu.VMEM((2, RADIX, RADIX), F32),
            pltpu.VMEM((1, RADIX), F32),
            *[pltpu.VMEM((2 * RADIX, 2 * RADIX), F32)] * 2,
            *[pltpu.VMEM((1, RADIX), F32)] * 2,
            pltpu.SemaphoreType.DMA((2,)),
            pltpu.SemaphoreType.DMA((GROUPS, 5)),
            pltpu.SemaphoreType.DMA((GROUPS, 10)),
            pltpu.SemaphoreType.DMA((GROUPS, SEGS)),
            pltpu.SemaphoreType.DMA((TABLES,)),
            *(pltpu.VMEM(table.shape, table.dtype) for table in tables),
        ],
        compiler_params=pltpu.CompilerParams(
            vmem_limit_bytes=VMEM_LIMIT, collective_id=0, has_side_effects=True
        ),
        name="matched_filter",
    )(strain.reshape(-1, 128), gate_mask.reshape(-1, 128), rows, *tables)


def whole(shape):
    return pl.BlockSpec(shape, lambda *_: (0,) * len(shape))


def local(strain, gate_mask, template_bank):
    template_total = template_bank.shape[0]
    count = lax.axis_size("seg")
    if count == SEGS and template_total == GROUP * GROUPS:
        return fused(strain, gate_mask, template_bank.reshape(template_total, -1, RADIX))
    gated = (strain * gate_mask.astype(F32)).reshape(-1, 128)
    pairs = [(i, i + 1) for i in range(count - 1)]
    prev = lax.ppermute(gated[-RADIX:], "seg", pairs)
    rows = template_bank.reshape(template_total, 2, -1, RADIX)
    bank = lax.all_gather(rows, "seg", axis=2, tiled=True)
    th, tl, fu = (jnp.asarray(t) for t in forward_tables())
    tables = [jnp.asarray(t) for t in inverse_tables()]
    params = pltpu.CompilerParams(vmem_limit_bytes=VMEM_LIMIT)
    spectra, gain = pl.pallas_call(
        forward_kernel,
        out_shape=(
            jax.ShapeDtypeStruct((2, RADIX, RADIX), F32),
            jax.ShapeDtypeStruct((1, RADIX), F32),
        ),
        compiler_params=params,
        name="window_spectra",
    )(gated, prev, th, tl, tables[2], fu)
    return pl.pallas_call(
        inverse_kernel,
        out_shape=jax.ShapeDtypeStruct((template_total, RADIX), F32),
        grid=(template_total,),
        in_specs=[
            pl.BlockSpec((1, 2, HALF, RADIX), lambda k: (k, 0, 0, 0)),
            whole((2, RADIX, RADIX)),
            whole((1, RADIX)),
            *(whole(t.shape) for t in tables),
        ],
        out_specs=whole((template_total, RADIX)),
        scratch_shapes=[pltpu.VMEM((2 * RADIX, 2 * RADIX), F32), pltpu.VMEM((1, RADIX), F32)],
        compiler_params=params,
        name="series_peaks",
    )(bank, spectra, gain, *tables)


def solution(mesh):
    in_specs = (P(("grp", "seg")), P(("grp", "seg")), P("grp", None, "seg"))
    out_specs = P(None, ("grp", "seg"))
    return jax.shard_map(local, mesh=mesh, in_specs=in_specs, out_specs=out_specs, check_vma=False)
```

```python
import functools
import math

import jax
import jax.numpy as jnp
import ml_dtypes
import numpy as np
from jax import lax
from jax.experimental import pallas as pl
from jax.experimental.pallas import tpu as pltpu
from jax.sharding import PartitionSpec as P

RADIX = 256
HALF = RADIX // 2
BLOCK = 32768
EPSILON = 1e-06
BF16 = jnp.bfloat16
F32 = jnp.float32
F8 = jnp.float8_e4m3fn
LIFT = 4096.0
NARROW = 16.0
SHRINK = 128.0
TOP = 16.0
MESH = pl.DeviceIdType.MESH
VMEM_LIMIT = 56 * 1024 * 1024
SEGS = 16
GROUP = 2
GROUPS = 4
CHIPS = 8
TABLES = 8


def angles(rows, cols, period):
    phase = np.outer(np.arange(rows), np.arange(cols)) % period
    turn = phase * (2.0 * math.pi / period)
    return np.cos(turn), np.sin(turn)


def two_parts(table):
    high = table.astype(ml_dtypes.bfloat16)
    low = (table - high.astype(np.float64)).astype(ml_dtypes.bfloat16)
    return high, low


@functools.cache
def forward_tables():
    cos, sin = angles(HALF, RADIX, RADIX)
    high, low = two_parts(np.concatenate([cos, -sin], axis=1))
    cos, sin = angles(HALF, RADIX, RADIX)
    second = two_parts(np.block([[cos, sin], [-sin, cos]]))
    return high, low, np.concatenate([second[0], second[1], second[0]], axis=1)


@functools.cache
def inverse_tables():
    cos, sin = angles(RADIX, HALF, RADIX)
    high, low = two_parts(np.block([[cos, -sin], [sin, cos]]))
    first = (high.astype(np.float64) * LIFT).astype(ml_dtypes.bfloat16)
    first_rest = np.concatenate([small(high.astype(np.float64) * NARROW), small(low.astype(np.float64) * LIFT)], axis=1)
    cos, sin = angles(RADIX, RADIX, RADIX * RADIX)
    twist = np.stack([cos, sin]).astype(np.float32)
    cos, sin = angles(RADIX, HALF, RADIX)
    high, low = two_parts(np.block([[cos, sin], [-sin, cos]]))
    second = (high.astype(np.float64) * LIFT).astype(ml_dtypes.bfloat16)
    second_rest = np.concatenate([small(high.astype(np.float64) * NARROW), small(low.astype(np.float64) * LIFT)], axis=0)
    return first, first_rest, twist, second, second_rest


def small(table):
    return table.astype(np.float64).astype(ml_dtypes.float8_e4m3fn)


def split(value):
    high = value.astype(BF16)
    return high, (value - high.astype(F32)).astype(BF16)


def split_small(value):
    high = value.astype(BF16)
    rest = ((value - high.astype(F32)) * (LIFT / NARROW)).astype(F8)
    return high, rest, value.astype(F8)


def dot(left, right):
    return jnp.dot(left, right, preferred_element_type=F32)


def inverse_kernel(h_ref, x_ref, gain_ref, t_ref, tr_ref, w_ref, u_ref, ur_ref, o_ref, part_ref, scale_ref):
    index = pl.program_id(0)
    bank_real, bank_imag = h_ref[0, 0].astype(F32), h_ref[0, 1].astype(F32)
    windows = [(x_ref[block, :HALF], x_ref[block, HALF:]) for block in range(2)]
    first_product(bank_real, bank_imag, windows, t_ref, tr_ref, part_ref, scale_ref)
    peaks = second_product(part_ref, scale_ref, gain_ref[:1], w_ref, u_ref, ur_ref)
    row = lax.broadcasted_iota(jnp.int32, o_ref.shape, 0)
    o_ref[...] = jnp.where(row == index, peaks, o_ref[...])


def first_product(bank_real, bank_imag, windows, t_ref, tr_ref, part_ref, scale_ref):
    scale = 1.0 / (BLOCK * jnp.sum(bank_real * bank_real + bank_imag * bank_imag) + EPSILON)
    scale_ref[...] = jnp.full(scale_ref.shape, scale, F32)
    pieces = []
    for real, imag in windows:
        pieces.append(
            split_small(
                jnp.concatenate(
                    [real * bank_real + imag * bank_imag, imag * bank_real - real * bank_imag],
                    axis=0,
                )
            )
        )
    high, rest, value = (jnp.concatenate(pair, axis=1) for pair in zip(*pieces))
    part_ref[...] = dot(t_ref[...], high) + dot(
        tr_ref[...], jnp.concatenate([rest, value], axis=0)
    )


def second_product(part_ref, scale_ref, gain, w_ref, u_ref, ur_ref):
    cos, sin = w_ref[0] * (1.0 / (LIFT * SHRINK)), w_ref[1] * (1.0 / (LIFT * SHRINK))
    pieces = []
    for block in range(2):
        columns = slice(block * RADIX, (block + 1) * RADIX)
        real, imag = part_ref[:RADIX, columns], part_ref[RADIX:, columns]
        high, rest, value = split_small(
            jnp.concatenate([real * cos - imag * sin, real * sin + imag * cos], axis=1)
        )
        pieces.append((high, jnp.concatenate([rest, value], axis=1)))
    high, small_parts = (jnp.concatenate(pair, axis=0) for pair in zip(*pieces))
    series = dot(high, u_ref[...]) + dot(small_parts, ur_ref[...])
    real, imag = series[:, :HALF], series[:, HALF:]
    power = real * real + imag * imag
    peaks = [
        jnp.max(power[block * RADIX : (block + 1) * RADIX], axis=0, keepdims=True)
        for block in range(2)
    ]
    both = jnp.concatenate(peaks, axis=1) * ((SHRINK / LIFT) ** 2 * scale_ref[...])
    return both * gain * gain


def window_spectra(grids, th_ref, tl_ref, w_ref, u_ref):
    def first_stage(grid):
        high, low = split(grid)
        return dot(high, th_ref[...]) + dot(low, th_ref[...]) + dot(high, tl_ref[...])

    parity = lax.broadcasted_iota(jnp.int32, (RADIX, 2 * RADIX), 1) % 2
    sign = (1 - 2 * parity).astype(F32)
    blocks = [first_stage(grid) for grid in grids]
    windows, gains = [], []
    for block in range(2):
        both = blocks[block + 1] + sign * blocks[block]
        real, imag = both[:, :RADIX], both[:, RADIX:]
        cos, sin = w_ref[0], w_ref[1]
        high, low = split(
            jnp.concatenate([real * cos + imag * sin, imag * cos - real * sin], axis=0)
        )
        spectra = dot(u_ref[...], jnp.concatenate([high, high, low], axis=0))
        gain = jnp.maximum(jnp.max(jnp.abs(spectra)), 1e-30) * (1.0 / TOP)
        gains.append(jnp.full((8, HALF), gain, F32))
        windows.append(spectra * (1.0 / gain))
    return windows, jnp.concatenate(gains, axis=1)


def grid_of(ref, start):
    halves = [ref[pl.ds(start + half, HALF, stride=2), :] for half in range(2)]
    return jnp.concatenate([half.T for half in halves], axis=0)


def forward_kernel(g_ref, prev_ref, th_ref, tl_ref, w_ref, u_ref, x_ref, gain_ref):
    grids = [grid_of(prev_ref, 0), grid_of(g_ref, 0), grid_of(g_ref, RADIX)]
    windows, gain_ref[...] = window_spectra(grids, th_ref, tl_ref, w_ref, u_ref)
    x_ref[0], x_ref[1] = windows


def fused_kernel(strain_ref, mask_ref, bank_ref, *refs):
    outside, refs = refs[:TABLES], refs[TABLES:]
    o_ref, gated, prev, held, x_ref, peak_ref, got_ref, part_a, part_b, scale_a, scale_b, *refs = refs
    prev_sem, swap_send, swap_recv, own_send, pass_send, recv_sem, side_sem, table_sem, *tables = refs
    th_ref, tl_ref, fu_ref, t_ref, tr_ref, w_ref, u_ref, ur_ref = tables
    me = lax.axis_index("seg")
    core, chip = me % 2, me // 2
    z_peers = [(me + 4 * step) % SEGS for step in range(1, 4)]
    z_chips = [(chip + 2 * step) % CHIPS for step in range(1, 4)]
    y_peer = me + 2 - 4 * (chip % 2)
    y_chips = [(chip + 1 - 2 * (chip % 2) + 2 * step) % CHIPS for step in range(4)]
    sibling = me + 1 - 2 * core
    last = SEGS - 1
    share = bank_ref.shape[0] // 2

    barrier = pltpu.get_barrier_semaphore()
    for peer in (*z_peers, y_peer, sibling, (me + last) % SEGS):
        pl.semaphore_signal(barrier, inc=1, device_id={"seg": peer}, device_id_type=MESH)

    table_copies = [
        pltpu.make_async_copy(outside[i], tables[i], table_sem.at[i]) for i in range(TABLES)
    ]
    for copy in table_copies:
        copy.start()
    gated[...] = strain_ref[...] * mask_ref[...].astype(F32)
    held[chip, :, core] = bank_ref[pl.ds(core * share, share)]

    pl.semaphore_wait(barrier, 6)

    def remote(source, target, send_sem, got_sem, peer):
        return pltpu.make_async_remote_copy(
            src_ref=source,
            dst_ref=target,
            send_sem=send_sem,
            recv_sem=got_sem,
            device_id={"seg": peer},
            device_id_type=MESH,
        )

    def prev_copy():
        tail = gated.at[pl.ds(RADIX, RADIX)]
        return remote(tail, prev, prev_sem.at[0], prev_sem.at[1], me + 1)

    def swap_copy(group):
        return remote(
            bank_ref.at[pl.ds((1 - core) * share + group * GROUP, GROUP)],
            held.at[chip, pl.ds(group * GROUP, GROUP), core],
            swap_send.at[group],
            swap_recv.at[group],
            sibling,
        )

    def chunk_copy(group, source, send_sem, peer):
        piece = held.at[source, pl.ds(group * GROUP, GROUP)]
        return remote(piece, piece, send_sem, recv_sem.at[group, source], peer)

    def own_copies(group):
        return [
            chunk_copy(group, chip, own_send.at[group, i], peer)
            for i, peer in enumerate((*z_peers, y_peer))
        ]

    def z_copies(group):
        return [
            chunk_copy(group, source, pass_send.at[group, i], y_peer)
            for i, source in enumerate(z_chips)
        ]

    def x_copy():
        return remote(x_ref.at[core], x_ref.at[core], side_sem.at[0], side_sem.at[1], sibling)

    def peak_copy():
        return remote(peak_ref.at[1 - core], got_ref, side_sem.at[2], side_sem.at[3], sibling)

    def own(group):
        swap_copy(group).wait_recv()
        for copy in own_copies(group):
            copy.start()

    def pass_z(group):
        for copy in z_copies(group):
            copy.wait_recv()
            copy.start()

    def all_arrived(group):
        for source in y_chips:
            chunk_copy(group, source, own_send.at[group, 0], y_peer).wait_recv()

    for group in range(GROUPS):
        swap_copy(group).start()

    @pl.when(me < last)
    def _():
        prev_copy().start()

    own(0)
    own(1)
    peak_ref[...] = jnp.zeros_like(peak_ref)

    @pl.when(me == 0)
    def _():
        prev[...] = jnp.zeros_like(prev)

    pass_z(0)

    @pl.when(me > 0)
    def _():
        prev_copy().wait_recv()

    own(2)
    for copy in table_copies:
        copy.wait()
    grids = [grid_of(prev, 0), grid_of(gated, 0), grid_of(gated, RADIX)]
    windows, gains = window_spectra(grids, th_ref, tl_ref, w_ref, fu_ref)
    x_ref[core] = jnp.concatenate([*windows, gains], axis=0)
    x_copy().start()
    pass_z(1)
    own(3)

    def first(template, side, part_ref, scale_ref):
        rows = held[:, template].astype(F32).reshape(SEGS, -1, RADIX)
        half = rows.shape[1] // 2
        bank_real = rows[:, :half].reshape(HALF, RADIX)
        bank_imag = rows[:, half:].reshape(HALF, RADIX)
        windows = [
            (x_ref[side, at : at + HALF], x_ref[side, at + HALF : at + RADIX]) for at in (0, RADIX)
        ]
        first_product(bank_real, bank_imag, windows, t_ref, tr_ref, part_ref, scale_ref)

    def second(template, side, part_ref, scale_ref):
        gain = x_ref[side, 2 * RADIX : 2 * RADIX + 1]
        peaks = second_product(part_ref, scale_ref, gain, w_ref, u_ref, ur_ref)
        row = lax.broadcasted_iota(jnp.int32, got_ref.shape, 0)
        peak_ref[side] = jnp.where(row == template, peaks, peak_ref[side])

    def pair(template, more):
        first(template, 1, part_b, scale_b)
        second(template, 0, part_a, scale_a)
        if more:
            first(template + 1, 0, part_a, scale_a)
        second(template, 1, part_b, scale_b)

    def step(group, carry):
        @pl.when(group + 2 < GROUPS)
        def _():
            pass_z(group + 2)

        pair(2 * group, True)
        all_arrived(group + 1)
        pair(2 * group + 1, True)
        return carry

    all_arrived(0)
    x_copy().wait_recv()
    first(0, 0, part_a, scale_a)
    lax.fori_loop(0, GROUPS - 1, step, 0)
    pair(2 * GROUPS - 2, True)
    pair(2 * GROUPS - 1, False)

    peak_copy().start()
    for group in range(GROUPS):
        for copy in (swap_copy(group), *own_copies(group), *z_copies(group)):
            copy.wait_send()
    x_copy().wait_send()

    @pl.when(me < last)
    def _():
        prev_copy().wait_send()

    peak_copy().wait()
    mine, other = peak_ref[core], got_ref[...]
    o_ref[:share] = jnp.where(core == 0, mine, other)
    o_ref[share:] = jnp.where(core == 0, other, mine)


def fused(strain, gate_mask, rows):
    template_total = rows.shape[0]
    tables = [jnp.asarray(t) for t in (*forward_tables(), *inverse_tables())]
    vmem = pl.BlockSpec(memory_space=pltpu.VMEM)
    return pl.pallas_call(
        fused_kernel,
        out_shape=jax.ShapeDtypeStruct((template_total, RADIX), F32),
        in_specs=[vmem] * 3 + [pl.BlockSpec(memory_space=pl.ANY)] * TABLES,
        out_specs=vmem,
        scratch_shapes=[
            pltpu.VMEM((2 * RADIX, 128), F32),
            pltpu.VMEM((RADIX, 128), F32),
            pltpu.VMEM((CHIPS, template_total // 2, 2, *rows.shape[1:]), BF16),
            pltpu.VMEM((2, 2 * RADIX + 8, RADIX), F32),
            pltpu.VMEM((2, template_total // 2, RADIX), F32),
            pltpu.VMEM((template_total // 2, RADIX), F32),
            *[pltpu.VMEM((2 * RADIX, 2 * RADIX), F32)] * 2,
            *[pltpu.VMEM((1, RADIX), F32)] * 2,
            pltpu.SemaphoreType.DMA((2,)),
            pltpu.SemaphoreType.DMA((GROUPS,)),
            pltpu.SemaphoreType.DMA((GROUPS,)),
            pltpu.SemaphoreType.DMA((GROUPS, 4)),
            pltpu.SemaphoreType.DMA((GROUPS, 3)),
            pltpu.SemaphoreType.DMA((GROUPS, CHIPS)),
            pltpu.SemaphoreType.DMA((4,)),
            pltpu.SemaphoreType.DMA((TABLES,)),
            *(pltpu.VMEM(table.shape, table.dtype) for table in tables),
        ],
        compiler_params=pltpu.CompilerParams(
            vmem_limit_bytes=VMEM_LIMIT, collective_id=0, has_side_effects=True
        ),
        name="matched_filter",
    )(strain.reshape(-1, 128), gate_mask.reshape(-1, 128), rows, *tables)


def whole(shape):
    return pl.BlockSpec(shape, lambda *_: (0,) * len(shape))


def local(strain, gate_mask, template_bank):
    template_total = template_bank.shape[0]
    count = lax.axis_size("seg")
    if count == SEGS and template_total == 2 * GROUP * GROUPS:
        return fused(strain, gate_mask, template_bank.reshape(template_total, -1, RADIX))
    gated = (strain * gate_mask.astype(F32)).reshape(-1, 128)
    pairs = [(i, i + 1) for i in range(count - 1)]
    prev = lax.ppermute(gated[-RADIX:], "seg", pairs)
    rows = template_bank.reshape(template_total, 2, -1, RADIX)
    bank = lax.all_gather(rows, "seg", axis=2, tiled=True)
    th, tl, fu = (jnp.asarray(t) for t in forward_tables())
    tables = [jnp.asarray(t) for t in inverse_tables()]
    params = pltpu.CompilerParams(vmem_limit_bytes=VMEM_LIMIT)
    spectra, gain = pl.pallas_call(
        forward_kernel,
        out_shape=(
            jax.ShapeDtypeStruct((2, RADIX, RADIX), F32),
            jax.ShapeDtypeStruct((8, RADIX), F32),
        ),
        compiler_params=params,
        name="window_spectra",
    )(gated, prev, th, tl, tables[2], fu)
    return pl.pallas_call(
        inverse_kernel,
        out_shape=jax.ShapeDtypeStruct((template_total, RADIX), F32),
        grid=(template_total,),
        in_specs=[
            pl.BlockSpec((1, 2, HALF, RADIX), lambda k: (k, 0, 0, 0)),
            whole((2, RADIX, RADIX)),
            whole((8, RADIX)),
            *(whole(t.shape) for t in tables),
        ],
        out_specs=whole((template_total, RADIX)),
        scratch_shapes=[pltpu.VMEM((2 * RADIX, 2 * RADIX), F32), pltpu.VMEM((1, RADIX), F32)],
        compiler_params=params,
        name="series_peaks",
    )(bank, spectra, gain, *tables)


def solution(mesh):
    in_specs = (P(("grp", "seg")), P(("grp", "seg")), P("grp", None, "seg"))
    out_specs = P(None, ("grp", "seg"))
    return jax.shard_map(local, mesh=mesh, in_specs=in_specs, out_specs=out_specs, check_vma=False)
```

```python
import functools
import math

import jax
import jax.numpy as jnp
import ml_dtypes
import numpy as np
from jax import lax
from jax.experimental import pallas as pl
from jax.experimental.pallas import tpu as pltpu
from jax.sharding import PartitionSpec as P

RADIX = 256
HALF = RADIX // 2
BLOCK = 32768
EPSILON = 1e-06
BF16 = jnp.bfloat16
F32 = jnp.float32
F8 = jnp.float8_e4m3fn
LIFT = 4096.0
NARROW = 16.0
SHRINK = 128.0
TOP = 16.0
ROWS = 32
MESH = pl.DeviceIdType.MESH
VMEM_LIMIT = 56 * 1024 * 1024
SEGS = 16
GROUP = 2
GROUPS = 4
CHIPS = 8
TABLES = 8
WORK = 5


def angles(rows, cols, period):
    phase = np.outer(np.arange(rows), np.arange(cols)) % period
    turn = phase * (2.0 * math.pi / period)
    return np.cos(turn), np.sin(turn)


def two_parts(table):
    high = table.astype(ml_dtypes.bfloat16)
    low = (table - high.astype(np.float64)).astype(ml_dtypes.bfloat16)
    return high, low


@functools.cache
def forward_tables():
    cos, sin = angles(HALF, RADIX, RADIX)
    high, low = two_parts(np.concatenate([cos, -sin], axis=1))
    cos, sin = angles(HALF, RADIX, RADIX)
    second = two_parts(np.block([[cos, sin], [-sin, cos]]))
    return high, low, np.concatenate([second[0], second[1], second[0]], axis=1)


@functools.cache
def inverse_tables():
    cos, sin = angles(RADIX, HALF, RADIX)
    high, low = two_parts(np.block([[cos, -sin], [sin, cos]]))
    first = (high.astype(np.float64) * LIFT).astype(ml_dtypes.bfloat16)
    first_rest = np.concatenate([small(high.astype(np.float64) * NARROW), small(low.astype(np.float64) * LIFT)], axis=1)
    cos, sin = angles(RADIX, RADIX, RADIX * RADIX)
    twist = np.stack([cos, sin]).astype(np.float32)
    cos, sin = angles(RADIX, HALF, RADIX)
    high, low = two_parts(np.block([[cos, sin], [-sin, cos]]))
    second = (high.astype(np.float64) * LIFT).astype(ml_dtypes.bfloat16)
    second_rest = np.concatenate([small(high.astype(np.float64) * NARROW), small(low.astype(np.float64) * LIFT)], axis=0)
    return first, first_rest, twist, second, second_rest


def small(table):
    return table.astype(np.float64).astype(ml_dtypes.float8_e4m3fn)


def split(value):
    high = value.astype(BF16)
    return high, (value - high.astype(F32)).astype(BF16)


def split_small(value):
    high = value.astype(BF16)
    rest = ((value - high.astype(F32)) * (LIFT / NARROW)).astype(F8)
    return high, rest, value.astype(F8)


def dot(left, right):
    return jnp.dot(left, right, preferred_element_type=F32)


def inverse_kernel(
    h_ref, x_ref, gain_ref, t_ref, tr_ref, w_ref, u_ref, ur_ref, o_ref, part_ref, scale_ref, *work
):
    def bank_tile(row, lane):
        spot = (pl.ds(row, ROWS), pl.ds(lane, 128))
        return h_ref[0, 0, *spot].astype(F32), h_ref[0, 1, *spot].astype(F32)

    def window_tile(block, row, lane):
        return x_ref[block, pl.ds(row, ROWS), pl.ds(lane, 128)]

    index = pl.program_id(0)
    first_product(bank_tile, window_tile, t_ref, tr_ref, part_ref, scale_ref, work)
    peaks = second_product(part_ref, scale_ref, gain_ref[:1], w_ref, u_ref, ur_ref, work)
    row = lax.broadcasted_iota(jnp.int32, o_ref.shape, 0)
    o_ref[...] = jnp.where(row == index, peaks, o_ref[...])


TILES = [(row, lane) for row in range(0, RADIX, ROWS) for lane in range(0, RADIX, 128)]


def first_product(bank_tile, window_tile, t_ref, tr_ref, part_ref, scale_ref, work):
    high_ref, rest_ref = work[:2]
    total = jnp.zeros((8, 128), F32)
    for row, lane in TILES:
        if row >= HALF:
            continue
        bank_real, bank_imag = bank_tile(row, lane)
        power = bank_real * bank_real + bank_imag * bank_imag
        total = total + jnp.sum(power.reshape(ROWS // 8, 8, 128), axis=0)
        for block in range(2):
            real, imag = window_tile(block, row, lane), window_tile(block, row + HALF, lane)
            columns = pl.ds(block * RADIX + lane, 128)
            values = (real * bank_real + imag * bank_imag, imag * bank_real - real * bank_imag)
            for at, value in zip((row, row + HALF), values):
                high, rest, value = split_small(value)
                high_ref[pl.ds(at, ROWS), columns] = high
                rest_ref[pl.ds(at, ROWS), columns] = rest
                rest_ref[pl.ds(at + RADIX, ROWS), columns] = value
    scale = 1.0 / (BLOCK * jnp.sum(total) + EPSILON)
    scale_ref[...] = jnp.full(scale_ref.shape, scale, F32)
    part_ref[0] = dot(t_ref[...], high_ref[...])
    part_ref[1] = dot(tr_ref[...], rest_ref[...])


def second_product(part_ref, scale_ref, gain, w_ref, u_ref, ur_ref, work):
    high_ref, rest_ref, series_ref = work[2:]
    for row, lane in TILES:
        spot = (pl.ds(row, ROWS), pl.ds(lane, 128))
        cos = w_ref[0, *spot] * (1.0 / (LIFT * SHRINK))
        sin = w_ref[1, *spot] * (1.0 / (LIFT * SHRINK))
        for block in range(2):
            columns = pl.ds(block * RADIX + lane, 128)
            real, imag = (
                part_ref[0, pl.ds(at, ROWS), columns] + part_ref[1, pl.ds(at, ROWS), columns]
                for at in (row, row + RADIX)
            )
            rows = pl.ds(block * RADIX + row, ROWS)
            values = (real * cos - imag * sin, real * sin + imag * cos)
            for at, value in zip((lane, lane + RADIX), values):
                high, rest, value = split_small(value)
                high_ref[rows, pl.ds(at, 128)] = high
                rest_ref[rows, pl.ds(at, 128)] = rest
                rest_ref[rows, pl.ds(at + 2 * RADIX, 128)] = value
    series_ref[0] = dot(high_ref[...], u_ref[...])
    series_ref[1] = dot(rest_ref[...], ur_ref[...])
    peaks = []
    for block in range(2):
        best = jnp.zeros((8, HALF), F32)
        for row in range(block * RADIX, (block + 1) * RADIX, ROWS):
            series = series_ref[0, pl.ds(row, ROWS)] + series_ref[1, pl.ds(row, ROWS)]
            real, imag = series[:, :HALF], series[:, HALF:]
            power = (real * real + imag * imag).reshape(ROWS // 8, 8, HALF)
            best = jnp.maximum(best, jnp.max(power, axis=0))
        peaks.append(jnp.max(best, axis=0, keepdims=True))
    both = jnp.concatenate(peaks, axis=1) * ((SHRINK / LIFT) ** 2 * scale_ref[...])
    return both * gain * gain


def part_scratch():
    return pltpu.VMEM((2, 2 * RADIX, 2 * RADIX), F32)


def work_scratch():
    return [
        pltpu.VMEM((RADIX, 2 * RADIX), BF16),
        pltpu.VMEM((2 * RADIX, 2 * RADIX), F8),
        pltpu.VMEM((2 * RADIX, 2 * RADIX), BF16),
        pltpu.VMEM((2 * RADIX, 4 * RADIX), F8),
        pltpu.VMEM((2, 2 * RADIX, RADIX), F32),
    ]


def window_spectra(grids, th_ref, tl_ref, w_ref, u_ref):
    def first_stage(grid):
        high, low = split(grid)
        return dot(high, th_ref[...]) + dot(low, th_ref[...]) + dot(high, tl_ref[...])

    parity = lax.broadcasted_iota(jnp.int32, (RADIX, 2 * RADIX), 1) % 2
    sign = (1 - 2 * parity).astype(F32)
    blocks = [first_stage(grid) for grid in grids]
    windows, gains = [], []
    for block in range(2):
        both = blocks[block + 1] + sign * blocks[block]
        real, imag = both[:, :RADIX], both[:, RADIX:]
        cos, sin = w_ref[0], w_ref[1]
        high, low = split(
            jnp.concatenate([real * cos + imag * sin, imag * cos - real * sin], axis=0)
        )
        spectra = dot(u_ref[...], jnp.concatenate([high, high, low], axis=0))
        gain = jnp.maximum(jnp.max(jnp.abs(spectra)), 1e-30) * (1.0 / TOP)
        gains.append(jnp.full((8, HALF), gain, F32))
        windows.append(spectra * (1.0 / gain))
    return windows, jnp.concatenate(gains, axis=1)


def grid_of(ref, start):
    halves = [ref[pl.ds(start + half, HALF, stride=2), :] for half in range(2)]
    return jnp.concatenate([half.T for half in halves], axis=0)


def forward_kernel(g_ref, prev_ref, th_ref, tl_ref, w_ref, u_ref, x_ref, gain_ref):
    grids = [grid_of(prev_ref, 0), grid_of(g_ref, 0), grid_of(g_ref, RADIX)]
    windows, gain_ref[...] = window_spectra(grids, th_ref, tl_ref, w_ref, u_ref)
    x_ref[0], x_ref[1] = windows


def fused_kernel(strain_ref, mask_ref, bank_ref, *refs):
    outside, refs = refs[:TABLES], refs[TABLES:]
    o_ref, gated, prev, held, x_ref, peak_ref, got_ref, part_a, part_b, scale_a, scale_b, *refs = refs
    work_a, work_b, refs = refs[:WORK], refs[WORK : 2 * WORK], refs[2 * WORK :]
    prev_sem, swap_send, swap_recv, own_send, pass_send, recv_sem, side_sem, table_sem, *tables = refs
    th_ref, tl_ref, fu_ref, t_ref, tr_ref, w_ref, u_ref, ur_ref = tables
    me = lax.axis_index("seg")
    core, chip = me % 2, me // 2
    z_peers = [(me + 4 * step) % SEGS for step in range(1, 4)]
    z_chips = [(chip + 2 * step) % CHIPS for step in range(1, 4)]
    y_peer = me + 2 - 4 * (chip % 2)
    y_chips = [(chip + 1 - 2 * (chip % 2) + 2 * step) % CHIPS for step in range(4)]
    sibling = me + 1 - 2 * core
    last = SEGS - 1
    share = bank_ref.shape[0] // 2

    barrier = pltpu.get_barrier_semaphore()
    for peer in (*z_peers, y_peer, sibling, (me + last) % SEGS):
        pl.semaphore_signal(barrier, inc=1, device_id={"seg": peer}, device_id_type=MESH)

    table_copies = [
        pltpu.make_async_copy(outside[i], tables[i], table_sem.at[i]) for i in range(TABLES)
    ]
    for copy in table_copies:
        copy.start()
    gated[...] = strain_ref[...] * mask_ref[...].astype(F32)
    held[chip, :, core] = bank_ref[pl.ds(core * share, share)]

    pl.semaphore_wait(barrier, 6)

    def remote(source, target, send_sem, got_sem, peer):
        return pltpu.make_async_remote_copy(
            src_ref=source,
            dst_ref=target,
            send_sem=send_sem,
            recv_sem=got_sem,
            device_id={"seg": peer},
            device_id_type=MESH,
        )

    def prev_copy():
        tail = gated.at[pl.ds(RADIX, RADIX)]
        return remote(tail, prev, prev_sem.at[0], prev_sem.at[1], me + 1)

    def swap_copy(group):
        return remote(
            bank_ref.at[pl.ds((1 - core) * share + group * GROUP, GROUP)],
            held.at[chip, pl.ds(group * GROUP, GROUP), core],
            swap_send.at[group],
            swap_recv.at[group],
            sibling,
        )

    def chunk_copy(group, source, send_sem, peer):
        piece = held.at[source, pl.ds(group * GROUP, GROUP)]
        return remote(piece, piece, send_sem, recv_sem.at[group, source], peer)

    def own_copies(group):
        return [
            chunk_copy(group, chip, own_send.at[group, i], peer)
            for i, peer in enumerate((*z_peers, y_peer))
        ]

    def z_copies(group):
        return [
            chunk_copy(group, source, pass_send.at[group, i], y_peer)
            for i, source in enumerate(z_chips)
        ]

    def x_copy():
        return remote(x_ref.at[core], x_ref.at[core], side_sem.at[0], side_sem.at[1], sibling)

    def peak_copy():
        return remote(peak_ref.at[1 - core], got_ref, side_sem.at[2], side_sem.at[3], sibling)

    def own(group):
        swap_copy(group).wait_recv()
        for copy in own_copies(group):
            copy.start()

    def pass_z(group):
        for copy in z_copies(group):
            copy.wait_recv()
            copy.start()

    def all_arrived(group):
        for source in y_chips:
            chunk_copy(group, source, own_send.at[group, 0], y_peer).wait_recv()

    for group in range(GROUPS):
        swap_copy(group).start()

    @pl.when(me < last)
    def _():
        prev_copy().start()

    own(0)
    own(1)
    peak_ref[...] = jnp.zeros_like(peak_ref)

    @pl.when(me == 0)
    def _():
        prev[...] = jnp.zeros_like(prev)

    pass_z(0)

    @pl.when(me > 0)
    def _():
        prev_copy().wait_recv()

    own(2)
    for copy in table_copies:
        copy.wait()
    grids = [grid_of(prev, 0), grid_of(gated, 0), grid_of(gated, RADIX)]
    windows, gains = window_spectra(grids, th_ref, tl_ref, w_ref, fu_ref)
    x_ref[core] = jnp.concatenate([*windows, gains], axis=0)
    x_copy().start()
    pass_z(1)
    own(3)

    def first(template, side, part_ref, scale_ref):
        def bank_tile(row, lane):
            chips = pl.ds(row // 16, ROWS // 16)
            rows = held[chips, template, :, :, pl.ds(lane, 128)].astype(F32)
            real, imag = rows[:, :, :8], rows[:, :, 8:]
            return real.reshape(ROWS, 128), imag.reshape(ROWS, 128)

        def window_tile(block, row, lane):
            return x_ref[side, pl.ds(block * RADIX + row, ROWS), pl.ds(lane, 128)]

        work = work_b if side else work_a
        first_product(bank_tile, window_tile, t_ref, tr_ref, part_ref, scale_ref, work)

    def second(template, side, part_ref, scale_ref):
        gain = x_ref[side, 2 * RADIX : 2 * RADIX + 1]
        work = work_b if side else work_a
        peaks = second_product(part_ref, scale_ref, gain, w_ref, u_ref, ur_ref, work)
        row = lax.broadcasted_iota(jnp.int32, got_ref.shape, 0)
        peak_ref[side] = jnp.where(row == template, peaks, peak_ref[side])

    def pair(template, more):
        first(template, 1, part_b, scale_b)
        second(template, 0, part_a, scale_a)
        if more:
            first(template + 1, 0, part_a, scale_a)
        second(template, 1, part_b, scale_b)

    def step(group, carry):
        @pl.when(group + 2 < GROUPS)
        def _():
            pass_z(group + 2)

        pair(2 * group, True)
        all_arrived(group + 1)
        pair(2 * group + 1, True)
        return carry

    all_arrived(0)
    x_copy().wait_recv()
    first(0, 0, part_a, scale_a)
    lax.fori_loop(0, GROUPS - 1, step, 0)
    pair(2 * GROUPS - 2, True)
    pair(2 * GROUPS - 1, False)

    peak_copy().start()
    for group in range(GROUPS):
        for copy in (swap_copy(group), *own_copies(group), *z_copies(group)):
            copy.wait_send()
    x_copy().wait_send()

    @pl.when(me < last)
    def _():
        prev_copy().wait_send()

    peak_copy().wait()
    mine, other = peak_ref[core], got_ref[...]
    o_ref[:share] = jnp.where(core == 0, mine, other)
    o_ref[share:] = jnp.where(core == 0, other, mine)


def fused(strain, gate_mask, rows):
    template_total = rows.shape[0]
    tables = [jnp.asarray(t) for t in (*forward_tables(), *inverse_tables())]
    vmem = pl.BlockSpec(memory_space=pltpu.VMEM)
    return pl.pallas_call(
        fused_kernel,
        out_shape=jax.ShapeDtypeStruct((template_total, RADIX), F32),
        in_specs=[vmem] * 3 + [pl.BlockSpec(memory_space=pl.ANY)] * TABLES,
        out_specs=vmem,
        scratch_shapes=[
            pltpu.VMEM((2 * RADIX, 128), F32),
            pltpu.VMEM((RADIX, 128), F32),
            pltpu.VMEM((CHIPS, template_total // 2, 2, *rows.shape[1:]), BF16),
            pltpu.VMEM((2, 2 * RADIX + 8, RADIX), F32),
            pltpu.VMEM((2, template_total // 2, RADIX), F32),
            pltpu.VMEM((template_total // 2, RADIX), F32),
            *[part_scratch()] * 2,
            *[pltpu.VMEM((1, RADIX), F32)] * 2,
            *work_scratch(),
            *work_scratch(),
            pltpu.SemaphoreType.DMA((2,)),
            pltpu.SemaphoreType.DMA((GROUPS,)),
            pltpu.SemaphoreType.DMA((GROUPS,)),
            pltpu.SemaphoreType.DMA((GROUPS, 4)),
            pltpu.SemaphoreType.DMA((GROUPS, 3)),
            pltpu.SemaphoreType.DMA((GROUPS, CHIPS)),
            pltpu.SemaphoreType.DMA((4,)),
            pltpu.SemaphoreType.DMA((TABLES,)),
            *(pltpu.VMEM(table.shape, table.dtype) for table in tables),
        ],
        compiler_params=pltpu.CompilerParams(
            vmem_limit_bytes=VMEM_LIMIT, collective_id=0, has_side_effects=True
        ),
        name="matched_filter",
    )(strain.reshape(-1, 128), gate_mask.reshape(-1, 128), rows, *tables)


def whole(shape):
    return pl.BlockSpec(shape, lambda *_: (0,) * len(shape))


def local(strain, gate_mask, template_bank):
    template_total = template_bank.shape[0]
    count = lax.axis_size("seg")
    if count == SEGS and template_total == 2 * GROUP * GROUPS:
        return fused(strain, gate_mask, template_bank.reshape(template_total, -1, RADIX))
    gated = (strain * gate_mask.astype(F32)).reshape(-1, 128)
    pairs = [(i, i + 1) for i in range(count - 1)]
    prev = lax.ppermute(gated[-RADIX:], "seg", pairs)
    rows = template_bank.reshape(template_total, 2, -1, RADIX)
    bank = lax.all_gather(rows, "seg", axis=2, tiled=True)
    th, tl, fu = (jnp.asarray(t) for t in forward_tables())
    tables = [jnp.asarray(t) for t in inverse_tables()]
    params = pltpu.CompilerParams(vmem_limit_bytes=VMEM_LIMIT)
    spectra, gain = pl.pallas_call(
        forward_kernel,
        out_shape=(
            jax.ShapeDtypeStruct((2, RADIX, RADIX), F32),
            jax.ShapeDtypeStruct((8, RADIX), F32),
        ),
        compiler_params=params,
        name="window_spectra",
    )(gated, prev, th, tl, tables[2], fu)
    return pl.pallas_call(
        inverse_kernel,
        out_shape=jax.ShapeDtypeStruct((template_total, RADIX), F32),
        grid=(template_total,),
        in_specs=[
            pl.BlockSpec((1, 2, HALF, RADIX), lambda k: (k, 0, 0, 0)),
            whole((2, RADIX, RADIX)),
            whole((8, RADIX)),
            *(whole(t.shape) for t in tables),
        ],
        out_specs=whole((template_total, RADIX)),
        scratch_shapes=[part_scratch(), pltpu.VMEM((1, RADIX), F32), *work_scratch()],
        compiler_params=params,
        name="series_peaks",
    )(bank, spectra, gain, *tables)


def solution(mesh):
    in_specs = (P(("grp", "seg")), P(("grp", "seg")), P("grp", None, "seg"))
    out_specs = P(None, ("grp", "seg"))
    return jax.shard_map(local, mesh=mesh, in_specs=in_specs, out_specs=out_specs, check_vma=False)
```
